32 devices in a mesh: ckpt: 2 (over x), tok: 16 (over z, y, core).
Axes of the slice: x: 2, y: 2, z: 4, core: 2. Of those that a mesh axis runs over, the one named last changes fastest.
Arguments:
- features: bfloat16 [2, 2048, 1792], P('ckpt', 'tok'), may hold values from -22 to 22
- pairing: int32 [2, 16, 128], P('ckpt', 'tok'), may hold values from 0 to 127, each once within a row
- rotation: bfloat16 [2, 1792, 1792], P('ckpt', 'tok'), may hold values from -1 to 2
Outputs:
- consensus: bfloat16 [2048, 1792], P('tok')
- rotation_next: bfloat16 [2, 1792, 1792], P('ckpt', 'tok')
The draws below stay inside these ranges and needn't reach their ends.
Inputs may be any that keep to these rules, and one draw needn't show every extreme that they name: Each row of a shard of 128 rows appears once in that shard's pairing.
All inputs are finite; a program needn't handle non-finite values.
Results may differ from the reference program's by a relative error of at most 0.011.
Values may be sent and summed in bfloat16 or wider, within the bound.
No kernel may reach another device: no remote copies, remote signals or barrier semaphores. Data moves between devices by JAX's collectives and lax.ppermute only.
A program may use at most 64 MiB of HBM per device.

```python
import math
import jax
import jax.numpy as jnp
from jax import lax

W = 1792
TOK_DEV = 128
CKPTS = 2
TOKENS = 2048
N_TOK = 16


def draw_features(key, part):
    base_key, column_key = jax.random.split(key, 2)
    columns = jnp.exp(0.5 * jax.random.uniform(column_key, (CKPTS, 1, W), jnp.float32, 0.0, math.log(10.0)))
    values = jnp.clip(jax.random.normal(base_key, (CKPTS, TOKENS, W), jnp.float32), -4.5, 4.5)
    return (values * columns).astype(jnp.bfloat16)


def draw_rotation(key, part):
    noise_key, diagonal_key = jax.random.split(key, 2)
    row_index = lax.broadcasted_iota(jnp.int32, (1, W, 1), 1)
    col_index = lax.broadcasted_iota(jnp.int32, (1, 1, W), 2)
    identity = (row_index == col_index).astype(jnp.float32)
    diagonal = jax.random.uniform(diagonal_key, (CKPTS, 1, W), jnp.float32, 0.75, 1.25)
    noise = jnp.clip(jax.random.normal(noise_key, (CKPTS, W, W), jnp.float32), -4.5, 4.5)
    return (identity * diagonal + 0.5 / math.sqrt(W) * noise).astype(jnp.bfloat16)


def setup_inputs(seed: int = 0) -> dict:
    key_of = jax.random.split(jax.random.key(seed), 4)
    features = draw_features(jax.random.fold_in(key_of[3], 71), 0)
    pairing = jax.vmap(lambda own: jax.random.permutation(own, TOK_DEV))(jax.random.split(key_of[1], CKPTS * N_TOK)).reshape((CKPTS, N_TOK, TOK_DEV)).astype(jnp.int32)
    rotation = draw_rotation(jax.random.fold_in(key_of[3], 71), 0)
    return dict(features=features, pairing=pairing, rotation=rotation)


def apply_once(vector, start_mat):
    inner = jnp.dot(vector.astype(jnp.bfloat16), start_mat.T, preferred_element_type=jnp.float32).astype(jnp.bfloat16)
    return jnp.dot(inner, start_mat, preferred_element_type=jnp.float32)

def reference(features, pairing, rotation):
    offsets = (jnp.arange(N_TOK, dtype=jnp.int32) * TOK_DEV)[:, None]
    aligned_list = []
    running = jnp.zeros((TOKENS, W), jnp.float32)
    for member in range(CKPTS):
        index = (pairing[member].astype(jnp.int32) + offsets).reshape(-1).astype(jnp.int32)
        aligned = jnp.take(features[member], index, axis=0)
        aligned_list.append(aligned)
        rotated = jnp.dot(aligned, rotation[member], preferred_element_type=jnp.float32).astype(jnp.bfloat16)
        running = running + rotated.astype(jnp.float32)
    consensus = (running / CKPTS).astype(jnp.bfloat16)
    results = []
    for member in range(CKPTS):
        cov = jnp.dot(aligned_list[member].T, consensus, preferred_element_type=jnp.float32)
        scale_now = 2.0 * jnp.sqrt(jnp.sum(cov * cov) / W + 1e-06)
        start_mat = (cov / scale_now).astype(jnp.bfloat16)
        first = 1.5 * start_mat.astype(jnp.float32) - 0.5 * apply_once(start_mat, start_mat)
        upper = 1.5 * first - 0.5 * apply_once(first, start_mat)
        middle = apply_once(upper, start_mat)
        cubic = 1.5 * middle - 0.5 * apply_once(middle, start_mat)
        results.append((math.sqrt(W) * (1.5 * first - 0.5 * cubic)).astype(jnp.bfloat16))
    return (consensus, jnp.stack(results, axis=0))
```

```python
import functools
import math

import jax
import jax.numpy as jnp
from jax import lax
from jax.experimental import pallas as pl
from jax.experimental.pallas import tpu as pltpu
from jax.sharding import PartitionSpec as P

BF16 = jnp.bfloat16
F32 = jnp.float32
VMEM = pl.BlockSpec(memory_space=pltpu.VMEM)
SMEM = pl.BlockSpec(memory_space=pltpu.SMEM)
PARAMS = pltpu.CompilerParams(vmem_limit_bytes=56 * 2**20)


def shape(dims, dtype):
    return jax.ShapeDtypeStruct(dims, dtype)


def contract(left, right, left_dim, right_dim):
    return lax.dot_general(
        left, right, (((left_dim,), (right_dim,)), ((), ())), preferred_element_type=F32
    )


def call(kernel, outs, smem, vmem, scratch=(), flops=0, nbytes=0):
    return pl.pallas_call(
        kernel,
        out_shape=outs,
        in_specs=[SMEM] * len(smem) + [VMEM] * len(vmem),
        out_specs=jax.tree.map(lambda _: VMEM, outs),
        scratch_shapes=list(scratch),
        compiler_params=PARAMS,
        cost_estimate=pl.CostEstimate(flops=flops, bytes_accessed=nbytes, transcendentals=0),
    )(*smem, *vmem)


def chip_at(position, chips):
    half = chips // 2
    return jnp.where(position < half, 2 * position, 2 * (chips - 1 - position) + 1)


def ring_pairs(chips):
    order = list(range(0, chips, 2)) + list(range(chips - 1, 0, -2))
    steps = [(order[i], order[(i + 1) % chips]) for i in range(chips)]
    up = [(a * 2 + core, b * 2 + core) for a, b in steps for core in (0, 1)]
    down = [(b, a) for a, b in up]
    last = [(a * 2, b * 2) for a, b in steps] + [(b * 2 + 1, a * 2 + 1) for a, b in steps]
    return up, down, last


def ring_gather(block, core, chips):
    up, down, last = ring_pairs(chips)
    blocks, ahead, behind = [block], block, block
    for _ in range(chips // 2 - 1):
        ahead = lax.ppermute(ahead, "tok", up)
        behind = lax.ppermute(behind, "tok", down)
        blocks += [ahead, behind]
    blocks.append(lax.ppermute(jnp.where(core == 0, ahead, behind), "tok", last))
    return blocks


def ring_offsets(chips):
    near = [sign * step for step in range(1, chips // 2) for sign in (-1, 1)]
    return [0] + near + [chips // 2]


def align_kernel(order_ref, rows_ref, out_ref):
    count = rows_ref.shape[0]
    picks = lax.broadcasted_iota(jnp.int32, (count, count), 0) == order_ref[...]
    out_ref[...] = contract(picks.astype(BF16), rows_ref[...], 0, 0).astype(BF16)


def rotate_kernel(count, *refs):
    blocks, cols_ref, out_ref = refs[:count], refs[count], refs[count + 1]
    for i, block in enumerate(blocks):
        out_ref[i] = jnp.dot(block[...], cols_ref[...], preferred_element_type=F32).astype(BF16)


def cov_kernel(count, members, *refs):
    blocks, parts = refs[:count], refs[count : count + members]
    cons_ref, cov_ref, rows_ref, all_ref = refs[count + members :]
    size = blocks[0].shape[0]
    for i, block in enumerate(blocks):
        total = parts[0][i].astype(F32)
        for part in parts[1:]:
            total = total + part[i].astype(F32)
        consensus = (total / members).astype(BF16)
        cons_ref[i] = consensus
        rows_ref[i * size : (i + 1) * size, :] = block[...]
        all_ref[i * size : (i + 1) * size, :] = consensus
    cov_ref[...] = contract(all_ref[...], rows_ref[...], 0, 0)


def chain_kernel(count, slab, *refs):
    where_ref, blocks = refs[0], refs[1 : count + 1]
    out_ref, whole, turned = refs[count + 1 :]
    width = whole.shape[0]
    size = width // count
    squares = jnp.zeros((1, width), F32)
    for i, block in enumerate(blocks):
        values = block[...]
        whole[i * size : (i + 1) * size, :] = values
        values = values.astype(F32)
        squares = squares + jnp.sum(values * values, axis=0, keepdims=True)
    inverse = 1.0 / (2.0 * jnp.sqrt(jnp.sum(squares, axis=1, keepdims=True) / width + 1e-06))

    rows = turned.shape[1]
    span = min(rows + 128, width)
    first_row = where_ref[count] * slab
    window = jnp.minimum(first_row // 128, (width - span) // 128) * 128
    window = pl.multiple_of(window, 128)
    columns = whole[:, pl.ds(window, span)]
    picks = lax.broadcasted_iota(jnp.int32, (rows, span), 1) == (
        lax.broadcasted_iota(jnp.int32, (rows, span), 0) + (first_row - window)
    )
    own = contract(picks.astype(BF16), columns, 1, 1)
    start = (own * inverse).astype(BF16)

    def apply_once(vector):
        inner = jnp.dot(vector.astype(BF16), whole[...], preferred_element_type=F32) * inverse
        return contract(inner.astype(BF16), whole[...], 1, 1) * inverse

    first = 1.5 * start.astype(F32) - 0.5 * apply_once(start)
    upper = 1.5 * first - 0.5 * apply_once(first)
    middle = apply_once(upper)
    cubic = 1.5 * middle - 0.5 * apply_once(middle)
    result = math.sqrt(width) * (1.5 * first - 0.5 * cubic)
    if count == 1:
        out_ref[...] = result[:slab].astype(BF16)
        return
    result = result.T
    for i in range(count):
        row = pl.multiple_of(where_ref[i] * size, 16)
        turned[pl.ds(row, size), :] = result[i * size : (i + 1) * size, :]
    out_ref[...] = turned[...].T[:slab].astype(BF16)


def shards(features, pairing, rotation):
    own_rows, own_order, rot_rows = features[0], pairing[0], rotation[0]
    count, width = own_rows.shape
    devices, members = lax.axis_size("tok"), lax.axis_size("ckpt")
    chips = devices // 2
    slab, cols = width // devices, width // chips
    index = lax.axis_index("tok")
    chip, core = index // 2, index % 2
    position = jnp.where(chip % 2 == 0, chip // 2, chips - 1 - chip // 2)
    siblings = [(i, i ^ 1) for i in range(devices)]
    parity = [[2 * i + c for i in range(chips)] for c in (0, 1)]
    pairs = [[2 * i, 2 * i + 1] for i in range(chips)]

    aligned = call(
        align_kernel, shape((count, width), BF16), [], [own_order, own_rows]
    )
    blocks = ring_gather(aligned, core, chips)

    rot_pieces = rot_rows.reshape(slab, chips, cols).transpose(1, 0, 2)
    rot_pieces = lax.all_to_all(
        rot_pieces, "tok", split_axis=0, concat_axis=0, tiled=True, axis_index_groups=parity
    )
    rot_cols = lax.all_gather(rot_pieces, "tok", axis=1, axis_index_groups=pairs).reshape(width, cols)

    rotated = call(
        functools.partial(rotate_kernel, chips),
        shape((chips, count, cols), BF16),
        [],
        blocks + [rot_cols],
        flops=2 * chips * count * cols * width,
        nbytes=2 * chips * count * width,
    )
    if members == 2:
        parts = [rotated, lax.ppermute(rotated, "ckpt", [(0, 1), (1, 0)])]
    else:
        gathered = lax.all_gather(rotated, "ckpt", axis=0)
        parts = [gathered[i] for i in range(members)]
    cons_blocks, cov = call(
        functools.partial(cov_kernel, chips, members),
        (shape((chips, count, cols), BF16), shape((cols, width), F32)),
        [],
        blocks + parts,
        [pltpu.VMEM((chips * count, width), BF16), pltpu.VMEM((chips * count, cols), BF16)],
        flops=2 * chips * count * cols * width,
        nbytes=2 * chips * count * width,
    )
    halves = cov.reshape(2, slab, width)
    keep = jnp.where(core == 0, halves[0], halves[1])
    give = jnp.where(core == 0, halves[1], halves[0]).astype(BF16)
    own = (keep + lax.ppermute(give, "tok", siblings).astype(F32)).astype(BF16)

    offsets = ring_offsets(chips)
    if slab % 16 == 0:
        same = ring_gather(own, core, chips)
        other = [lax.ppermute(block, "tok", siblings) for block in same]
        at = [chip_at((position + offset) % chips, chips) * 2 for offset in offsets]
        places = [a + core for a in at] + [a + 1 - core for a in at]
        gathered = same + other
    else:
        places = [jnp.zeros_like(index)]
        gathered = [lax.all_gather(own, "tok", axis=0, tiled=True)]
    rows = -(-slab // 128) * 128
    rotation_next = call(
        functools.partial(chain_kernel, len(gathered), slab),
        shape((slab, width), BF16),
        [jnp.stack(places + [index]).astype(jnp.int32)],
        gathered,
        [pltpu.VMEM((width, width), BF16), pltpu.VMEM((width, rows), F32)],
        flops=16 * rows * width * width,
        nbytes=2 * width * width,
    )

    natural = jnp.stack([chip_at((position + offset) % chips, chips) for offset in offsets])
    ordered = jnp.zeros_like(cons_blocks).at[natural].set(cons_blocks, unique_indices=True)
    consensus = lax.all_to_all(
        ordered, "tok", split_axis=0, concat_axis=0, tiled=True, axis_index_groups=parity
    )
    consensus = consensus.transpose(1, 0, 2).reshape(count, width)
    return (consensus, rotation_next[None])


def solution(mesh):
    placed = (P("ckpt", "tok", None), P("ckpt", "tok", None), P("ckpt", "tok", None))
    return jax.shard_map(
        shards,
        mesh=mesh,
        in_specs=placed,
        out_specs=(P("tok", None), P("ckpt", "tok", None)),
        check_vma=False,
    )
```

```python
import functools
import math

import jax
import jax.numpy as jnp
from jax import lax
from jax.experimental import pallas as pl
from jax.experimental.pallas import tpu as pltpu
from jax.sharding import PartitionSpec as P

BF16 = jnp.bfloat16
F32 = jnp.float32
VMEM = pl.BlockSpec(memory_space=pltpu.VMEM)
SMEM = pl.BlockSpec(memory_space=pltpu.SMEM)


def shape(dims, dtype):
    return jax.ShapeDtypeStruct(dims, dtype)


def contract(left, right, left_dim, right_dim):
    return lax.dot_general(
        left, right, (((left_dim,), (right_dim,)), ((), ())), preferred_element_type=F32
    )


def nbytes(array):
    return math.prod(array.shape) * jnp.dtype(array.dtype).itemsize


def call(kernel, outs, smem, vmem, scratch=(), flops=0, room=4):
    held = sum(map(nbytes, [*vmem, *jax.tree.leaves(outs), *scratch]))
    return pl.pallas_call(
        kernel,
        out_shape=outs,
        in_specs=[SMEM] * len(smem) + [VMEM] * len(vmem),
        out_specs=jax.tree.map(lambda _: VMEM, outs),
        scratch_shapes=[pltpu.VMEM(s.shape, s.dtype) for s in scratch],
        compiler_params=pltpu.CompilerParams(vmem_limit_bytes=held + room * 2**20),
        cost_estimate=pl.CostEstimate(flops=flops, bytes_accessed=held, transcendentals=0),
    )(*smem, *vmem)


def position_of(chip, chips):
    return jnp.where(chip % 2 == 0, chip // 2, chips - 1 - chip // 2)


def chip_at(position, chips):
    return jnp.where(position < chips // 2, 2 * position, 2 * (chips - 1 - position) + 1)


def me(chips):
    index = lax.axis_index("tok")
    return index, index % 2, position_of(index // 2, chips)


def ring_order(chips):
    return list(range(0, chips, 2)) + list(range(chips - 1, 0, -2))


def shift(block, by, chips):
    order = ring_order(chips)
    pairs = [(order[i], order[(i + by) % chips]) for i in range(chips)]
    return lax.ppermute(block, "tok", [(2 * a + c, 2 * b + c) for a, b in pairs for c in (0, 1)])


def ring_gather(halves, chips):
    blocks, ahead, behind = [list(halves)], list(halves), list(halves)
    for _ in range(chips // 2 - 1):
        for i in range(2):
            ahead[i] = shift(ahead[i], 1, chips)
            behind[i] = shift(behind[i], -1, chips)
        blocks += [list(ahead), list(behind)]
    blocks.append([shift(ahead[0], 1, chips), shift(behind[1], -1, chips)])
    return blocks


def ring_offsets(chips):
    near = [sign * step for step in range(1, chips // 2) for sign in (-1, 1)]
    return [0] + near + [chips // 2]


def align_kernel(order_ref, rows_ref, out_ref):
    count = rows_ref.shape[0]
    picks = lax.broadcasted_iota(jnp.int32, (count, count), 0) == order_ref[...]
    out_ref[...] = contract(picks.astype(BF16), rows_ref[...], 0, 0).astype(BF16)


def pieces_kernel(chips, rows_ref, *refs):
    outs, held = refs[:chips], refs[chips]
    _, _, position = me(chips)
    cols = held.shape[2]
    for chip in range(chips):
        held[chip] = rows_ref[:, chip * cols : (chip + 1) * cols]
    for out, offset in zip(outs, ring_offsets(chips), strict=True):
        out[...] = held[chip_at((position + offset + chips) % chips, chips)]


def stack_kernel(chips, *refs):
    pieces, out_ref = refs[:chips], refs[chips]
    _, _, position = me(chips)
    slab = pieces[0].shape[0]
    for piece, offset in zip(pieces, ring_offsets(chips), strict=True):
        chip = chip_at((position - offset + chips) % chips, chips)
        out_ref[pl.ds(pl.multiple_of(chip * slab, 16), slab), :] = piece[...]


def join_kernel(chips, *refs):
    pieces, out_ref, held = refs[:chips], refs[chips], refs[chips + 1]
    _, _, position = me(chips)
    cols = held.shape[2]
    for piece, offset in zip(pieces, ring_offsets(chips), strict=True):
        held[chip_at((position - offset + chips) % chips, chips)] = piece[...]
    for chip in range(chips):
        out_ref[:, chip * cols : (chip + 1) * cols] = held[chip]


def rotate_kernel(count, chips, *refs):
    halves = refs[:count]
    size = halves[0].shape[0]
    if len(refs) == count + 2:
        cols_ref, out_ref = refs[count:]
    else:
        own_ref, sibling_ref, out_ref, cols_ref = refs[count:]
        _, core, _ = me(chips)
        slab = own_ref.shape[0] // chips
        for chip in range(chips):
            for ref, parity in ((own_ref, core), (sibling_ref, 1 - core)):
                row = pl.multiple_of((2 * chip + parity) * slab, 16)
                cols_ref[pl.ds(row, slab), :] = ref[chip * slab : (chip + 1) * slab, :]
    for i, half in enumerate(halves):
        out_ref[i * size : (i + 1) * size, :] = jnp.dot(
            half[...], cols_ref[...], preferred_element_type=F32
        ).astype(BF16)


def cov_sum(halves, groups, cons_ref, rows_ref):
    size = halves[0].shape[0]
    for i, half in enumerate(halves):
        rows_ref[i * size : (i + 1) * size, :] = half[...]
    at = 0
    for parts in groups:
        total = parts[0][...].astype(F32)
        for part in parts[1:]:
            total = total + part[...].astype(F32)
        cons_ref[at : at + total.shape[0], :] = (total / len(parts)).astype(BF16)
        at += total.shape[0]
    return contract(cons_ref[...], rows_ref[...], 0, 0)


def early_kernel(count, members, *refs):
    halves, parts = refs[:count], refs[count : count + members]
    cons_ref, cov_ref, rows_ref = refs[count + members :]
    cov_ref[...] = cov_sum(halves, [parts], cons_ref, rows_ref)


def late_kernel(count, members, *refs):
    core = lax.axis_index("tok") % 2
    halves, middle = refs[:count], refs[count : count + members]
    far = refs[count + members : count + 2 * members]
    early_ref, cons_ref, keep_ref, give_ref, rows_ref = refs[count + 2 * members :]
    cov = early_ref[...] + cov_sum(halves, [middle, far], cons_ref, rows_ref)
    slab = cov.shape[0] // 2
    low, high = cov[:slab], cov[slab:]
    keep_ref[...] = jnp.where(core == 0, low, high)
    give_ref[...] = jnp.where(core == 0, high, low).astype(BF16)


def chain_kernel(count, slab, *refs):
    blocks = refs[: 2 * count]
    out_ref, whole, turned = refs[2 * count :]
    width = whole.shape[0]
    chips = width // slab // 2
    index, core, position = me(chips)
    size, half = width // count, width // 2
    squares = jnp.zeros((1, width), F32)
    for i in range(count):
        for side in range(2):
            whole[i * size : (i + 1) * size, side * half : (side + 1) * half] = blocks[2 * i + side][...]
        values = whole[i * size : (i + 1) * size, :].astype(F32)
        squares = squares + jnp.sum(values * values, axis=0, keepdims=True)
    inverse = 1.0 / (2.0 * jnp.sqrt(jnp.sum(squares, axis=1, keepdims=True) / width + 1e-06))

    rows = turned.shape[1]
    span = min(rows + 128, width)
    first_row = index * slab
    window = jnp.minimum(first_row // 128, (width - span) // 128) * 128
    window = pl.multiple_of(window, 128)
    columns = whole[:, pl.ds(window, span)]
    picks = lax.broadcasted_iota(jnp.int32, (rows, span), 1) == (
        lax.broadcasted_iota(jnp.int32, (rows, span), 0) + (first_row - window)
    )
    own = contract(picks.astype(BF16), columns, 1, 1)
    start = (own * inverse).astype(BF16)

    def apply_once(vector):
        inner = jnp.dot(vector.astype(BF16), whole[...], preferred_element_type=F32) * inverse
        return contract(inner.astype(BF16), whole[...], 1, 1) * inverse

    first = 1.5 * start.astype(F32) - 0.5 * apply_once(start)
    upper = 1.5 * first - 0.5 * apply_once(first)
    middle = apply_once(upper)
    cubic = 1.5 * middle - 0.5 * apply_once(middle)
    result = math.sqrt(width) * (1.5 * first - 0.5 * cubic)
    if count == 1:
        out_ref[...] = result[:slab].astype(BF16)
        return
    result = result.T
    for i in range(count):
        chip = chip_at((position + ring_offsets(chips)[i % chips] + chips) % chips, chips)
        parity = core if i < chips else 1 - core
        row = pl.multiple_of((2 * chip + parity) * size, 16)
        turned[pl.ds(row, size), :] = result[i * size : (i + 1) * size, :]
    out_ref[...] = turned[...].T[:slab].astype(BF16)


def shards(features, pairing, rotation):
    own_rows, own_order, rot_rows = features[0], pairing[0], rotation[0]
    count, width = own_rows.shape
    devices, members = lax.axis_size("tok"), lax.axis_size("ckpt")
    chips = devices // 2
    slab, cols = width // devices, width // chips
    siblings = [(i, i ^ 1) for i in range(devices)]
    parity = [[2 * i + c for i in range(chips)] for c in (0, 1)]
    pairs = [[2 * i, 2 * i + 1] for i in range(chips)]
    offsets = ring_offsets(chips)
    tiled = slab % 16 == 0

    aligned = call(align_kernel, shape((count, width), BF16), [], [own_order, own_rows])
    blocks = ring_gather(jnp.split(aligned, 2, axis=0), chips)

    if tiled:
        pieces = call(
            functools.partial(pieces_kernel, chips),
            [shape((slab, cols), BF16)] * chips,
            [],
            [rot_rows],
            [shape((chips, slab, cols), BF16)],
        )
        pieces = [pieces[0]] + [
            shift(piece, offset, chips) for piece, offset in zip(pieces[1:], offsets[1:], strict=True)
        ]
        stacked = call(
            functools.partial(stack_kernel, chips), shape((chips * slab, cols), BF16), [], pieces
        )
        rot_cols = [stacked, lax.ppermute(stacked, "tok", siblings)]
        rot_scratch = [shape((width, cols), BF16)]
    else:
        pieces = rot_rows.reshape(slab, chips, cols).transpose(1, 0, 2)
        pieces = lax.all_to_all(
            pieces, "tok", split_axis=0, concat_axis=0, tiled=True, axis_index_groups=parity
        )
        pieces = lax.all_gather(pieces, "tok", axis=1, axis_index_groups=pairs)
        rot_cols, rot_scratch = [pieces.reshape(width, cols)], []

    def rotate(group):
        halves = sum(group, [])
        rotated = call(
            functools.partial(rotate_kernel, len(halves), chips),
            shape((len(group) * count, cols), BF16),
            [],
            halves + rot_cols,
            rot_scratch,
            flops=2 * len(group) * count * cols * width,
        )
        if members == 2:
            return halves, [rotated, lax.ppermute(rotated, "ckpt", [(0, 1), (1, 0)])]
        gathered = lax.all_gather(rotated, "ckpt", axis=0)
        return halves, [gathered[i] for i in range(members)]

    early_rows, early_parts = rotate(blocks[:-3])
    middle_rows, middle_parts = rotate(blocks[-3:-1])
    far_rows, far_parts = rotate(blocks[-1:])
    near = (chips - 3) * count
    early_cons, early_cov = call(
        functools.partial(early_kernel, len(early_rows), members),
        (shape((near, cols), BF16), shape((cols, width), F32)),
        [],
        early_rows + early_parts,
        [shape((near, width), BF16)],
        flops=2 * near * cols * width,
    )
    late_rows = middle_rows + far_rows
    late_cons, keep, give = call(
        functools.partial(late_kernel, len(late_rows), members),
        (shape((3 * count, cols), BF16), shape((slab, width), F32), shape((slab, width), BF16)),
        [],
        late_rows + middle_parts + far_parts + [early_cov],
        [shape((3 * count, width), BF16)],
        flops=2 * 3 * count * cols * width,
    )
    own = (keep + lax.ppermute(give, "tok", siblings).astype(F32)).astype(BF16)

    if tiled:
        same = ring_gather(jnp.split(own, 2, axis=1), chips)
        other = [[lax.ppermute(half, "tok", siblings) for half in block] for block in same]
        gathered = sum(same + other, [])
    else:
        gathered = jnp.split(lax.all_gather(own, "tok", axis=0, tiled=True), 2, axis=1)
    rows = -(-slab // 128) * 128
    rotation_next = call(
        functools.partial(chain_kernel, len(gathered) // 2, slab),
        shape((slab, width), BF16),
        [],
        gathered,
        [shape((width, width), BF16), shape((width, rows), F32)],
        flops=16 * rows * width * width,
        room=10,
    )

    cons = [early_cons[i : i + count] for i in range(0, near, count)]
    cons += [late_cons[i : i + count] for i in range(0, 3 * count, count)]
    if tiled:
        cons = cons[:1] + [
            shift(block, offset, chips) for block, offset in zip(cons[1:], offsets[1:], strict=True)
        ]
        consensus = call(
            functools.partial(join_kernel, chips),
            shape((count, width), BF16),
            [],
            cons,
            [shape((chips, count, cols), BF16)],
        )
    else:
        _, _, position = me(chips)
        natural = jnp.stack([chip_at((position + offset + chips) % chips, chips) for offset in offsets])
        ordered = jnp.zeros((chips, count, cols), BF16).at[natural].set(jnp.stack(cons), unique_indices=True)
        consensus = lax.all_to_all(
            ordered, "tok", split_axis=0, concat_axis=0, tiled=True, axis_index_groups=parity
        )
        consensus = consensus.transpose(1, 0, 2).reshape(count, width)
    return (consensus, rotation_next[None])


def solution(mesh):
    placed = (P("ckpt", "tok", None), P("ckpt", "tok", None), P("ckpt", "tok", None))
    return jax.shard_map(
        shards,
        mesh=mesh,
        in_specs=placed,
        out_specs=(P("tok", None), P("ckpt", "tok", None)),
        check_vma=False,
    )
```

```python
import functools
import math

import jax
import jax.numpy as jnp
from jax import lax
from jax.experimental import pallas as pl
from jax.experimental.pallas import tpu as pltpu
from jax.sharding import PartitionSpec as P

BF16 = jnp.bfloat16
F32 = jnp.float32
STREAMS = ((1, 0), (1, 1), (-1, 0), (-1, 1))
VMEM = pl.BlockSpec(memory_space=pltpu.VMEM)
SMEM = pl.BlockSpec(memory_space=pltpu.SMEM)


def shape(dims, dtype):
    return jax.ShapeDtypeStruct(dims, dtype)


def contract(left, right, left_dim, right_dim):
    return lax.dot_general(
        left, right, (((left_dim,), (right_dim,)), ((), ())), preferred_element_type=F32
    )


def nbytes(array):
    return math.prod(array.shape) * jnp.dtype(array.dtype).itemsize


def call(kernel, outs, smem, vmem, scratch=(), flops=0, room=4):
    held = sum(map(nbytes, [*vmem, *jax.tree.leaves(outs), *scratch]))
    return pl.pallas_call(
        kernel,
        out_shape=outs,
        in_specs=[SMEM] * len(smem) + [VMEM] * len(vmem),
        out_specs=jax.tree.map(lambda _: VMEM, outs),
        scratch_shapes=[pltpu.VMEM(s.shape, s.dtype) for s in scratch],
        compiler_params=pltpu.CompilerParams(vmem_limit_bytes=held + room * 2**20),
        cost_estimate=pl.CostEstimate(flops=flops, bytes_accessed=held, transcendentals=0),
    )(*smem, *vmem)


def position_of(chip, chips):
    return jnp.where(chip % 2 == 0, chip // 2, chips - 1 - chip // 2)


def chip_at(position, chips):
    return jnp.where(position < chips // 2, 2 * position, 2 * (chips - 1 - position) + 1)


def me(chips):
    index = lax.axis_index("tok")
    return index, index % 2, position_of(index // 2, chips)


def ring_order(chips):
    return list(range(0, chips, 2)) + list(range(chips - 1, 0, -2))


def shift(block, by, chips):
    order = ring_order(chips)
    pairs = [(order[i], order[(i + by) % chips]) for i in range(chips)]
    return lax.ppermute(block, "tok", [(2 * a + c, 2 * b + c) for a, b in pairs for c in (0, 1)])


def ring_gather(halves, chips):
    blocks, ahead, behind = [list(halves)], list(halves), list(halves)
    for _ in range(chips // 2 - 1):
        for i in range(2):
            ahead[i] = shift(ahead[i], 1, chips)
            behind[i] = shift(behind[i], -1, chips)
        blocks += [list(ahead), list(behind)]
    blocks.append([shift(ahead[0], 1, chips), shift(behind[1], -1, chips)])
    return blocks


def halve_kernel(ahead_ref, behind_ref, upper_ref, lower_ref):
    half = upper_ref.shape[0]
    upper_ref[...] = ahead_ref[:half]
    lower_ref[...] = behind_ref[half:]


def ring_whole(block, chips):
    blocks, ahead, behind = [[block]], block, block
    for _ in range(chips // 2 - 1):
        ahead, behind = shift(ahead, 1, chips), shift(behind, -1, chips)
        blocks += [[ahead], [behind]]
    rows, width = block.shape
    upper, lower = call(halve_kernel, [shape((rows // 2, width), BF16)] * 2, [], [ahead, behind])
    blocks.append([shift(upper, 1, chips), shift(lower, -1, chips)])
    return blocks


def tie(arrays, others):
    return lax.optimization_barrier((arrays, others))[0]


def ring_offsets(chips):
    near = [sign * step for step in range(1, chips // 2) for sign in (-1, 1)]
    return [0] + near + [chips // 2]


def align_kernel(order_ref, rows_ref, out_ref):
    count = rows_ref.shape[0]
    picks = lax.broadcasted_iota(jnp.int32, (count, count), 0) == order_ref[...]
    out_ref[...] = contract(picks.astype(BF16), rows_ref[...], 0, 0).astype(BF16)


def cut_kernel(chips, rows_ref, out_ref):
    cols = out_ref.shape[2]
    for chip in range(chips):
        out_ref[chip] = rows_ref[:, chip * cols : (chip + 1) * cols]


def fold(rows, groups):
    size = rows.shape[0] // groups
    return [rows[i * size : (i + 1) * size] for i in range(groups)]


def pack_kernel(chips, count, keep_ref, come_ref, early_ref, late_ref, *outs):
    first_ref, second_ref, *streams = outs
    slab, half = first_ref.shape
    groups, offsets = chips // 2, ring_offsets(chips)
    own = (keep_ref[...] + come_ref[...].astype(F32)).astype(BF16)
    cols = half // groups
    blocks = [early_ref[i : i + count] for i in range(0, early_ref.shape[0], count)]
    blocks += [late_ref[i : i + count] for i in range(0, late_ref.shape[0], count)]
    for ref, (sign, side) in zip(streams, STREAMS, strict=True):
        ref[:slab] = own[:, side * half : (side + 1) * half]
        last = chips // 2 if (sign == 1) == (side == 0) else chips // 2 - 1
        row = slab
        for step in range(last, 0, -1):
            block = blocks[offsets.index(sign * step if step < chips // 2 else step)]
            parts = fold(block[side * count // 2 : (side + 1) * count // 2], groups)
            for i, part in enumerate(parts):
                ref[row : row + part.shape[0], i * cols : (i + 1) * cols] = part
            row += parts[0].shape[0]
    first_ref[...] = own[:, :half]
    second_ref[...] = own[:, half:]


def trim_kernel(message_ref, block_ref, piece_ref, *rest_ref):
    slab, size = block_ref.shape[0], piece_ref.shape[0]
    rest = message_ref.shape[0] - size
    block_ref[...] = message_ref[:slab]
    piece_ref[...] = message_ref[rest:]
    for ref in rest_ref:
        ref[...] = message_ref[:rest]


def join_kernel(chips, slab, places, first_ref, *refs):
    pieces, out_ref, held = refs[:-2], refs[-2], refs[-1]
    _, _, position = me(chips)
    count, cols = held.shape[1:]
    groups = chips // 2
    size = count // 2 // groups
    held[chip_at(position, chips)] = first_ref[...]
    for ref, (offset, side) in zip(pieces, places, strict=True):
        chip = chip_at((position + offset + chips) % chips, chips)
        piece = ref[ref.shape[0] - size :]
        for j in range(groups):
            base = side * count // 2 + j * size
            held[chip, base : base + size, :] = piece[:, j * cols : (j + 1) * cols]
    for chip in range(chips):
        out_ref[:, chip * cols : (chip + 1) * cols] = held[chip]


def rotate_kernel(count, chips, *refs):
    halves = refs[:count]
    if len(refs) == count + 2:
        cols_ref, out_ref = refs[count:]
    else:
        own_ref, sibling_ref, out_ref, cols_ref = refs[count:]
        _, core, _ = me(chips)
        slab = own_ref.shape[0] // chips
        for chip in range(chips):
            for ref, parity in ((own_ref, core), (sibling_ref, 1 - core)):
                row = pl.multiple_of((2 * chip + parity) * slab, 16)
                cols_ref[pl.ds(row, slab), :] = ref[chip * slab : (chip + 1) * slab, :]
    at = 0
    for half in halves:
        out_ref[at : at + half.shape[0], :] = jnp.dot(
            half[...], cols_ref[...], preferred_element_type=F32
        ).astype(BF16)
        at += half.shape[0]


def cov_sum(halves, groups, cons_ref, rows_ref):
    at = 0
    for half in halves:
        rows_ref[at : at + half.shape[0], :] = half[...]
        at += half.shape[0]
    at = 0
    for parts in groups:
        total = parts[0][...].astype(F32)
        for part in parts[1:]:
            total = total + part[...].astype(F32)
        cons_ref[at : at + total.shape[0], :] = (total / len(parts)).astype(BF16)
        at += total.shape[0]
    return contract(cons_ref[...], rows_ref[...], 0, 0)


def early_kernel(count, members, *refs):
    halves, parts = refs[:count], refs[count : count + members]
    cons_ref, cov_ref, rows_ref = refs[count + members :]
    cov_ref[...] = cov_sum(halves, [parts], cons_ref, rows_ref)


def late_kernel(count, members, *refs):
    core = lax.axis_index("tok") % 2
    halves, middle = refs[:count], refs[count : count + members]
    far = refs[count + members : count + 2 * members]
    early_ref, cons_ref, keep_ref, give_ref, rows_ref = refs[count + 2 * members :]
    cov = early_ref[...] + cov_sum(halves, [middle, far], cons_ref, rows_ref)
    slab = cov.shape[0] // 2
    low, high = cov[:slab], cov[slab:]
    keep_ref[...] = jnp.where(core == 0, low, high)
    give_ref[...] = jnp.where(core == 0, high, low).astype(BF16)


def chain_kernel(count, slab, *refs):
    blocks = refs[: 2 * count]
    out_ref, whole, turned = refs[2 * count :]
    width = whole.shape[0]
    chips = width // slab // 2
    index, core, position = me(chips)
    size, half = width // count, width // 2
    squares = jnp.zeros((1, width), F32)
    for i in range(count):
        for side in range(2):
            whole[i * size : (i + 1) * size, side * half : (side + 1) * half] = blocks[2 * i + side][:size]
        values = whole[i * size : (i + 1) * size, :].astype(F32)
        squares = squares + jnp.sum(values * values, axis=0, keepdims=True)
    inverse = 1.0 / (2.0 * jnp.sqrt(jnp.sum(squares, axis=1, keepdims=True) / width + 1e-06))

    rows = turned.shape[1]
    span = min(rows + 128, width)
    first_row = index * slab
    window = jnp.minimum(first_row // 128, (width - span) // 128) * 128
    window = pl.multiple_of(window, 128)
    columns = whole[:, pl.ds(window, span)]
    picks = lax.broadcasted_iota(jnp.int32, (rows, span), 1) == (
        lax.broadcasted_iota(jnp.int32, (rows, span), 0) + (first_row - window)
    )
    own = contract(picks.astype(BF16), columns, 1, 1)
    start = (own * inverse).astype(BF16)

    def apply_once(vector):
        inner = jnp.dot(vector.astype(BF16), whole[...], preferred_element_type=F32) * inverse
        return contract(inner.astype(BF16), whole[...], 1, 1) * inverse

    first = 1.5 * start.astype(F32) - 0.5 * apply_once(start)
    upper = 1.5 * first - 0.5 * apply_once(first)
    middle = apply_once(upper)
    cubic = 1.5 * middle - 0.5 * apply_once(middle)
    result = math.sqrt(width) * (1.5 * first - 0.5 * cubic)
    if count == 1:
        out_ref[...] = result[:slab].astype(BF16)
        return
    result = result.T
    for i in range(count):
        chip = chip_at((position + ring_offsets(chips)[i % chips] + chips) % chips, chips)
        parity = core if i < chips else 1 - core
        row = pl.multiple_of((2 * chip + parity) * size, 16)
        turned[pl.ds(row, size), :] = result[i * size : (i + 1) * size, :]
    out_ref[...] = turned[...].T[:slab].astype(BF16)


def shards(features, pairing, rotation):
    own_rows, own_order, rot_rows = features[0], pairing[0], rotation[0]
    count, width = own_rows.shape
    devices, members = lax.axis_size("tok"), lax.axis_size("ckpt")
    chips = devices // 2
    slab, cols = width // devices, width // chips
    siblings = [(i, i ^ 1) for i in range(devices)]
    parity = [[2 * i + c for i in range(chips)] for c in (0, 1)]
    pairs = [[2 * i, 2 * i + 1] for i in range(chips)]
    offsets = ring_offsets(chips)
    tiled = slab % 16 == 0 and count % (16 * chips) == 0

    aligned = call(align_kernel, shape((count, width), BF16), [], [own_order, own_rows])
    blocks = ring_whole(aligned, chips)

    pieces = call(
        functools.partial(cut_kernel, chips), shape((chips, slab, cols), BF16), [], [rot_rows]
    )
    pieces = lax.all_to_all(
        pieces, "tok", split_axis=0, concat_axis=0, tiled=True, axis_index_groups=parity
    )
    if tiled:
        stacked = pieces.reshape(chips * slab, cols)
        rot_cols = [stacked, lax.ppermute(stacked, "tok", siblings)]
        rot_scratch = [shape((width, cols), BF16)]
    else:
        pieces = lax.all_gather(pieces, "tok", axis=1, axis_index_groups=pairs)
        rot_cols, rot_scratch = [pieces.reshape(width, cols)], []

    def rotate(group):
        halves = sum(group, [])
        rotated = call(
            functools.partial(rotate_kernel, len(halves), chips),
            shape((len(group) * count, cols), BF16),
            [],
            halves + rot_cols,
            rot_scratch,
            flops=2 * len(group) * count * cols * width,
        )
        if members == 2:
            return halves, [rotated, lax.ppermute(rotated, "ckpt", [(0, 1), (1, 0)])]
        gathered = lax.all_gather(rotated, "ckpt", axis=0)
        return halves, [gathered[i] for i in range(members)]

    early_rows, early_parts = rotate(blocks[:-3])
    middle_rows, middle_parts = rotate(blocks[-3:-1])
    far_rows, far_parts = rotate(blocks[-1:])
    near = (chips - 3) * count
    early_cons, early_cov = call(
        functools.partial(early_kernel, len(early_rows), members),
        (shape((near, cols), BF16), shape((cols, width), F32)),
        [],
        early_rows + early_parts,
        [shape((near, width), BF16)],
        flops=2 * near * cols * width,
    )
    late_rows = middle_rows + far_rows
    late_cons, keep, give = call(
        functools.partial(late_kernel, len(late_rows), members),
        (shape((3 * count, cols), BF16), shape((slab, width), F32), shape((slab, width), BF16)),
        [],
        late_rows + middle_parts + far_parts + [early_cov],
        [shape((3 * count, width), BF16)],
        flops=2 * 3 * count * cols * width,
    )
    come = lax.ppermute(give, "tok", siblings)

    if tiled:
        half, last = width // 2, chips // 2 - 1
        size = count // chips
        sizes = [slab + size * (last + (sign == 1) * (side == 0) + (sign == -1) * (side == 1)) for sign, side in STREAMS]
        first, second, *streams = call(
            functools.partial(pack_kernel, chips, count),
            [shape((slab, half), BF16)] * 2 + [shape((rows, half), BF16) for rows in sizes],
            [],
            [keep, come, early_cons, late_cons],
        )
        same, pieces, places = [[first, second]], [], []
        for step in range(1, last + 1):
            parts = []
            for i, (sign, side) in enumerate(STREAMS):
                message = shift(streams[i], sign, chips)
                outs = [shape((rows, half), BF16) for rows in (slab, size, message.shape[0] - size)]
                if outs[2].shape == outs[0].shape:
                    outs = outs[:2]
                block, piece, *rest = call(trim_kernel, outs, [], [message])
                streams[i] = rest[0] if rest else block
                parts.append(block)
                pieces.append(piece)
                places.append((-sign * step, side))
            same += [parts[:2], parts[2:]]
        far = [shift(streams[0], 1, chips), shift(streams[3], -1, chips)]
        same.append(far)
        pieces += far
        places += [(chips // 2, 0), (chips // 2, 1)]
        other = [[lax.ppermute(part, "tok", siblings) for part in block] for block in same]
        gathered = sum(same + other, [])
    else:
        own = (keep + come.astype(F32)).astype(BF16)
        gathered = jnp.split(lax.all_gather(own, "tok", axis=0, tiled=True), 2, axis=1)
    rows = -(-slab // 128) * 128
    rotation_next = call(
        functools.partial(chain_kernel, len(gathered) // 2, slab),
        shape((slab, width), BF16),
        [],
        gathered,
        [shape((width, width), BF16), shape((width, rows), F32)],
        flops=16 * rows * width * width,
        room=10,
    )

    if tiled:
        consensus = call(
            functools.partial(join_kernel, chips, slab, places),
            shape((count, width), BF16),
            [],
            [early_cons[:count]] + pieces,
            [shape((chips, count, cols), BF16)],
        )
    else:
        cons = jnp.concatenate([early_cons, late_cons]).reshape(chips, count, cols)
        _, _, position = me(chips)
        natural = jnp.stack([chip_at((position + offset + chips) % chips, chips) for offset in offsets])
        ordered = jnp.zeros((chips, count, cols), BF16).at[natural].set(cons, unique_indices=True)
        consensus = lax.all_to_all(
            ordered, "tok", split_axis=0, concat_axis=0, tiled=True, axis_index_groups=parity
        )
        consensus = consensus.transpose(1, 0, 2).reshape(count, width)
    return (consensus, rotation_next[None])


def solution(mesh):
    placed = (P("ckpt", "tok", None), P("ckpt", "tok", None), P("ckpt", "tok", None))
    return jax.shard_map(
        shards,
        mesh=mesh,
        in_specs=placed,
        out_specs=(P("tok", None), P("ckpt", "tok", None)),
        check_vma=False,
    )
```

```python
import functools
import math

import jax
import jax.numpy as jnp
from jax import lax
from jax.experimental import pallas as pl
from jax.experimental.pallas import tpu as pltpu
from jax.sharding import PartitionSpec as P

BF16 = jnp.bfloat16
F32 = jnp.float32
STREAMS = ((1, 0), (1, 1), (-1, 0), (-1, 1))
VMEM = pl.BlockSpec(memory_space=pltpu.VMEM)
SMEM = pl.BlockSpec(memory_space=pltpu.SMEM)


def shape(dims, dtype):
    return jax.ShapeDtypeStruct(dims, dtype)


def contract(left, right, left_dim, right_dim):
    return lax.dot_general(
        left, right, (((left_dim,), (right_dim,)), ((), ())), preferred_element_type=F32
    )


def nbytes(array):
    return math.prod(array.shape) * jnp.dtype(array.dtype).itemsize


def call(kernel, outs, smem, vmem, scratch=(), flops=0, room=4):
    held = sum(map(nbytes, [*vmem, *jax.tree.leaves(outs), *scratch]))
    return pl.pallas_call(
        kernel,
        out_shape=outs,
        in_specs=[SMEM] * len(smem) + [VMEM] * len(vmem),
        out_specs=jax.tree.map(lambda _: VMEM, outs),
        scratch_shapes=[pltpu.VMEM(s.shape, s.dtype) for s in scratch],
        compiler_params=pltpu.CompilerParams(vmem_limit_bytes=held + room * 2**20),
        cost_estimate=pl.CostEstimate(flops=flops, bytes_accessed=held, transcendentals=0),
    )(*smem, *vmem)


def position_of(chip, chips):
    return jnp.where(chip % 2 == 0, chip // 2, chips - 1 - chip // 2)


def chip_at(position, chips):
    return jnp.where(position < chips // 2, 2 * position, 2 * (chips - 1 - position) + 1)


def me(chips):
    index = lax.axis_index("tok")
    return index, index % 2, position_of(index // 2, chips)


def ring_order(chips):
    return list(range(0, chips, 2)) + list(range(chips - 1, 0, -2))


def shift(block, by, chips):
    order = ring_order(chips)
    pairs = [(order[i], order[(i + by) % chips]) for i in range(chips)]
    return lax.ppermute(block, "tok", [(2 * a + c, 2 * b + c) for a, b in pairs for c in (0, 1)])


def ring_gather(halves, chips):
    blocks, ahead, behind = [list(halves)], list(halves), list(halves)
    for _ in range(chips // 2 - 1):
        for i in range(2):
            ahead[i] = shift(ahead[i], 1, chips)
            behind[i] = shift(behind[i], -1, chips)
        blocks += [list(ahead), list(behind)]
    blocks.append([shift(ahead[0], 1, chips), shift(behind[1], -1, chips)])
    return blocks


def halve_kernel(ahead_ref, behind_ref, upper_ref, lower_ref):
    half = upper_ref.shape[0]
    upper_ref[...] = ahead_ref[:half]
    lower_ref[...] = behind_ref[half:]


def ring_whole(block, chips):
    blocks, ahead, behind = [[block]], block, block
    for _ in range(chips // 2 - 1):
        ahead, behind = shift(ahead, 1, chips), shift(behind, -1, chips)
        blocks += [[ahead], [behind]]
    rows, width = block.shape
    upper, lower = call(halve_kernel, [shape((rows // 2, width), BF16)] * 2, [], [ahead, behind])
    blocks.append([shift(upper, 1, chips), shift(lower, -1, chips)])
    return blocks


def tie(arrays, others):
    return lax.optimization_barrier((arrays, others))[0]


def ring_offsets(chips):
    near = [sign * step for step in range(1, chips // 2) for sign in (-1, 1)]
    return [0] + near + [chips // 2]


def align_kernel(order_ref, rows_ref, out_ref):
    count = rows_ref.shape[0]
    picks = lax.broadcasted_iota(jnp.int32, (count, count), 0) == order_ref[...]
    out_ref[...] = contract(picks.astype(BF16), rows_ref[...], 0, 0).astype(BF16)


def cut_kernel(chips, rows_ref, out_ref):
    cols = out_ref.shape[2]
    for chip in range(chips):
        out_ref[chip] = rows_ref[:, chip * cols : (chip + 1) * cols]


def fold(rows, groups):
    size = rows.shape[0] // groups
    return [rows[i * size : (i + 1) * size] for i in range(groups)]


def pack_kernel(chips, count, keep_ref, come_ref, early_ref, late_ref, *outs):
    first_ref, second_ref, *streams = outs
    slab, half = first_ref.shape
    groups, offsets = chips // 2, ring_offsets(chips)
    own = (keep_ref[...] + come_ref[...].astype(F32)).astype(BF16)
    cols = half // groups
    blocks = [early_ref[i : i + count] for i in range(0, early_ref.shape[0], count)]
    blocks += [late_ref[i : i + count] for i in range(0, late_ref.shape[0], count)]
    for ref, (sign, side) in zip(streams, STREAMS, strict=True):
        ref[:slab] = own[:, side * half : (side + 1) * half]
        last = chips // 2 if (sign == 1) == (side == 0) else chips // 2 - 1
        row = slab
        for step in range(last, 0, -1):
            block = blocks[offsets.index(sign * step if step < chips // 2 else step)]
            parts = fold(block[side * count // 2 : (side + 1) * count // 2], groups)
            for i, part in enumerate(parts):
                ref[row : row + part.shape[0], i * cols : (i + 1) * cols] = part
            row += parts[0].shape[0]
    first_ref[...] = own[:, :half]
    second_ref[...] = own[:, half:]


def trim_kernel(message_ref, block_ref, piece_ref, *rest_ref):
    slab, size = block_ref.shape[0], piece_ref.shape[0]
    rest = message_ref.shape[0] - size
    block_ref[...] = message_ref[:slab]
    piece_ref[...] = message_ref[rest:]
    for ref in rest_ref:
        ref[...] = message_ref[:rest]


def join_kernel(chips, slab, places, first_ref, *refs):
    pieces, out_ref, held = refs[:-2], refs[-2], refs[-1]
    _, _, position = me(chips)
    count, cols = held.shape[1:]
    groups = chips // 2
    size = count // 2 // groups
    held[chip_at(position, chips)] = first_ref[...]
    for ref, (offset, side) in zip(pieces, places, strict=True):
        chip = chip_at((position + offset + chips) % chips, chips)
        piece = ref[ref.shape[0] - size :]
        for j in range(groups):
            base = side * count // 2 + j * size
            held[chip, base : base + size, :] = piece[:, j * cols : (j + 1) * cols]
    for chip in range(chips):
        out_ref[:, chip * cols : (chip + 1) * cols] = held[chip]


def rotate_kernel(count, chips, *refs):
    halves = refs[:count]
    if len(refs) == count + 2:
        cols_ref, out_ref = refs[count:]
    else:
        own_ref, sibling_ref, out_ref, cols_ref = refs[count:]
        _, core, _ = me(chips)
        slab = own_ref.shape[0] // chips
        for chip in range(chips):
            for ref, parity in ((own_ref, core), (sibling_ref, 1 - core)):
                row = pl.multiple_of((2 * chip + parity) * slab, 16)
                cols_ref[pl.ds(row, slab), :] = ref[chip * slab : (chip + 1) * slab, :]
    at = 0
    for half in halves:
        out_ref[at : at + half.shape[0], :] = jnp.dot(
            half[...], cols_ref[...], preferred_element_type=F32
        ).astype(BF16)
        at += half.shape[0]


def cov_sum(halves, groups, cons_ref, rows_ref):
    at = 0
    for half in halves:
        rows_ref[at : at + half.shape[0], :] = half[...]
        at += half.shape[0]
    at = 0
    for parts in groups:
        total = parts[0][...].astype(F32)
        for part in parts[1:]:
            total = total + part[...].astype(F32)
        cons_ref[at : at + total.shape[0], :] = (total / len(parts)).astype(BF16)
        at += total.shape[0]
    return contract(cons_ref[...], rows_ref[...], 0, 0)


def early_kernel(count, members, *refs):
    halves, parts = refs[:count], refs[count : count + members]
    cons_ref, cov_ref, rows_ref = refs[count + members :]
    cov_ref[...] = cov_sum(halves, [parts], cons_ref, rows_ref)


def late_kernel(count, members, *refs):
    core = lax.axis_index("tok") % 2
    halves, middle = refs[:count], refs[count : count + members]
    far = refs[count + members : count + 2 * members]
    early_ref, cons_ref, keep_ref, give_ref, rows_ref = refs[count + 2 * members :]
    cov = early_ref[...] + cov_sum(halves, [middle, far], cons_ref, rows_ref)
    slab = cov.shape[0] // 2
    low, high = cov[:slab], cov[slab:]
    keep_ref[...] = jnp.where(core == 0, low, high)
    give_ref[...] = jnp.where(core == 0, high, low).astype(BF16)


def chain_kernel(count, slab, *refs):
    blocks = refs[: 2 * count]
    out_ref, whole, flipped, turned = refs[2 * count :]
    width = whole.shape[0]
    chips = width // slab // 2
    index, core, position = me(chips)
    size, half = width // count, width // 2
    squares = jnp.zeros((1, width), F32)
    for i in range(count):
        for side in range(2):
            whole[i * size : (i + 1) * size, side * half : (side + 1) * half] = blocks[2 * i + side][:size]
        values = whole[i * size : (i + 1) * size, :].astype(F32)
        squares = squares + jnp.sum(values * values, axis=0, keepdims=True)
    inverse = 1.0 / (2.0 * jnp.sqrt(jnp.sum(squares, axis=1, keepdims=True) / width + 1e-06))

    rows = turned.shape[1]
    span = min(rows + 128, width)
    first_row = index * slab
    window = jnp.minimum(first_row // 128, (width - span) // 128) * 128
    window = pl.multiple_of(window, 128)
    columns = whole[:, pl.ds(window, span)]
    picks = lax.broadcasted_iota(jnp.int32, (rows, span), 1) == (
        lax.broadcasted_iota(jnp.int32, (rows, span), 0) + (first_row - window)
    )
    own = contract(picks.astype(BF16), columns, 1, 1)
    start = (own * inverse).astype(BF16)

    flipped[...] = whole[...].T

    def apply_once(vector):
        inner = jnp.dot(vector.astype(BF16), whole[...], preferred_element_type=F32) * inverse
        return jnp.dot(inner.astype(BF16), flipped[...], preferred_element_type=F32) * inverse

    first = 1.5 * start.astype(F32) - 0.5 * apply_once(start)
    upper = 1.5 * first - 0.5 * apply_once(first)
    middle = apply_once(upper)
    cubic = 1.5 * middle - 0.5 * apply_once(middle)
    result = math.sqrt(width) * (1.5 * first - 0.5 * cubic)
    if count == 1:
        out_ref[...] = result[:slab].astype(BF16)
        return
    result = result.T
    for i in range(count):
        chip = chip_at((position + ring_offsets(chips)[i % chips] + chips) % chips, chips)
        parity = core if i < chips else 1 - core
        row = pl.multiple_of((2 * chip + parity) * size, 16)
        turned[pl.ds(row, size), :] = result[i * size : (i + 1) * size, :]
    out_ref[...] = turned[...].T[:slab].astype(BF16)


def shards(features, pairing, rotation):
    own_rows, own_order, rot_rows = features[0], pairing[0], rotation[0]
    count, width = own_rows.shape
    devices, members = lax.axis_size("tok"), lax.axis_size("ckpt")
    chips = devices // 2
    slab, cols = width // devices, width // chips
    siblings = [(i, i ^ 1) for i in range(devices)]
    parity = [[2 * i + c for i in range(chips)] for c in (0, 1)]
    pairs = [[2 * i, 2 * i + 1] for i in range(chips)]
    offsets = ring_offsets(chips)
    tiled = slab % 16 == 0 and count % (16 * chips) == 0

    aligned = call(align_kernel, shape((count, width), BF16), [], [own_order, own_rows])
    blocks = ring_whole(aligned, chips)

    pieces = call(
        functools.partial(cut_kernel, chips), shape((chips, slab, cols), BF16), [], [rot_rows]
    )
    pieces = lax.all_to_all(
        pieces, "tok", split_axis=0, concat_axis=0, tiled=True, axis_index_groups=parity
    )
    if tiled:
        stacked = pieces.reshape(chips * slab, cols)
        rot_cols = [stacked, lax.ppermute(stacked, "tok", siblings)]
        rot_scratch = [shape((width, cols), BF16)]
    else:
        pieces = lax.all_gather(pieces, "tok", axis=1, axis_index_groups=pairs)
        rot_cols, rot_scratch = [pieces.reshape(width, cols)], []

    def rotate(group):
        halves = sum(group, [])
        rotated = call(
            functools.partial(rotate_kernel, len(halves), chips),
            shape((len(group) * count, cols), BF16),
            [],
            halves + rot_cols,
            rot_scratch,
            flops=2 * len(group) * count * cols * width,
        )
        if members == 2:
            return halves, [rotated, lax.ppermute(rotated, "ckpt", [(0, 1), (1, 0)])]
        gathered = lax.all_gather(rotated, "ckpt", axis=0)
        return halves, [gathered[i] for i in range(members)]

    early_rows, early_parts = rotate(blocks[:-3])
    middle_rows, middle_parts = rotate(blocks[-3:-1])
    far_rows, far_parts = rotate(blocks[-1:])
    near = (chips - 3) * count
    early_cons, early_cov = call(
        functools.partial(early_kernel, len(early_rows), members),
        (shape((near, cols), BF16), shape((cols, width), F32)),
        [],
        early_rows + early_parts,
        [shape((near, width), BF16)],
        flops=2 * near * cols * width,
    )
    late_rows = middle_rows + far_rows
    late_cons, keep, give = call(
        functools.partial(late_kernel, len(late_rows), members),
        (shape((3 * count, cols), BF16), shape((slab, width), F32), shape((slab, width), BF16)),
        [],
        late_rows + middle_parts + far_parts + [early_cov],
        [shape((3 * count, width), BF16)],
        flops=2 * 3 * count * cols * width,
    )
    come = lax.ppermute(give, "tok", siblings)

    if tiled:
        half, last = width // 2, chips // 2 - 1
        size = count // chips
        sizes = [slab + size * (last + (sign == 1) * (side == 0) + (sign == -1) * (side == 1)) for sign, side in STREAMS]
        first, second, *streams = call(
            functools.partial(pack_kernel, chips, count),
            [shape((slab, half), BF16)] * 2 + [shape((rows, half), BF16) for rows in sizes],
            [],
            [keep, come, early_cons, late_cons],
        )
        same, pieces, places = [[first, second]], [], []
        for step in range(1, last + 1):
            parts = []
            for i, (sign, side) in enumerate(STREAMS):
                message = shift(streams[i], sign, chips)
                outs = [shape((rows, half), BF16) for rows in (slab, size, message.shape[0] - size)]
                if outs[2].shape == outs[0].shape:
                    outs = outs[:2]
                block, piece, *rest = call(trim_kernel, outs, [], [message])
                streams[i] = rest[0] if rest else block
                parts.append(block)
                pieces.append(piece)
                places.append((-sign * step, side))
            same += [parts[:2], parts[2:]]
        far = [shift(streams[0], 1, chips), shift(streams[3], -1, chips)]
        same.append(far)
        pieces += far
        places += [(chips // 2, 0), (chips // 2, 1)]
        other = [[lax.ppermute(part, "tok", siblings) for part in block] for block in same]
        gathered = sum(same + other, [])
    else:
        own = (keep + come.astype(F32)).astype(BF16)
        gathered = jnp.split(lax.all_gather(own, "tok", axis=0, tiled=True), 2, axis=1)
    rows = -(-slab // 128) * 128
    rotation_next = call(
        functools.partial(chain_kernel, len(gathered) // 2, slab),
        shape((slab, width), BF16),
        [],
        gathered,
        [shape((width, width), BF16)] * 2 + [shape((width, rows), F32)],
        flops=16 * rows * width * width,
        room=10,
    )

    if tiled:
        consensus = call(
            functools.partial(join_kernel, chips, slab, places),
            shape((count, width), BF16),
            [],
            [early_cons[:count]] + pieces,
            [shape((chips, count, cols), BF16)],
        )
    else:
        cons = jnp.concatenate([early_cons, late_cons]).reshape(chips, count, cols)
        _, _, position = me(chips)
        natural = jnp.stack([chip_at((position + offset + chips) % chips, chips) for offset in offsets])
        ordered = jnp.zeros((chips, count, cols), BF16).at[natural].set(cons, unique_indices=True)
        consensus = lax.all_to_all(
            ordered, "tok", split_axis=0, concat_axis=0, tiled=True, axis_index_groups=parity
        )
        consensus = consensus.transpose(1, 0, 2).reshape(count, width)
    return (consensus, rotation_next[None])


def solution(mesh):
    placed = (P("ckpt", "tok", None), P("ckpt", "tok", None), P("ckpt", "tok", None))
    return jax.shard_map(
        shards,
        mesh=mesh,
        in_specs=placed,
        out_specs=(P("tok", None), P("ckpt", "tok", None)),
        check_vma=False,
    )
```

```python
import functools
import math

import jax
import jax.numpy as jnp
from jax import lax
from jax.experimental import pallas as pl
from jax.experimental.pallas import tpu as pltpu
from jax.sharding import PartitionSpec as P

BF16 = jnp.bfloat16
F32 = jnp.float32
STREAMS = ((1, 0), (1, 1), (-1, 0), (-1, 1))
VMEM = pl.BlockSpec(memory_space=pltpu.VMEM)
SMEM = pl.BlockSpec(memory_space=pltpu.SMEM)


def shape(dims, dtype):
    return jax.ShapeDtypeStruct(dims, dtype)


def contract(left, right, left_dim, right_dim):
    return lax.dot_general(
        left, right, (((left_dim,), (right_dim,)), ((), ())), preferred_element_type=F32
    )


def nbytes(array):
    return math.prod(array.shape) * jnp.dtype(array.dtype).itemsize


def call(kernel, outs, smem, vmem, scratch=(), flops=0, room=4):
    held = sum(map(nbytes, [*vmem, *jax.tree.leaves(outs), *scratch]))
    return pl.pallas_call(
        kernel,
        out_shape=outs,
        in_specs=[SMEM] * len(smem) + [VMEM] * len(vmem),
        out_specs=jax.tree.map(lambda _: VMEM, outs),
        scratch_shapes=[pltpu.VMEM(s.shape, s.dtype) for s in scratch],
        compiler_params=pltpu.CompilerParams(vmem_limit_bytes=held + room * 2**20),
        cost_estimate=pl.CostEstimate(flops=flops, bytes_accessed=held, transcendentals=0),
    )(*smem, *vmem)


def position_of(chip, chips):
    return jnp.where(chip % 2 == 0, chip // 2, chips - 1 - chip // 2)


def chip_at(position, chips):
    return jnp.where(position < chips // 2, 2 * position, 2 * (chips - 1 - position) + 1)


def me(chips):
    index = lax.axis_index("tok")
    return index, index % 2, position_of(index // 2, chips)


def ring_order(chips):
    return list(range(0, chips, 2)) + list(range(chips - 1, 0, -2))


def shift(block, by, chips):
    order = ring_order(chips)
    pairs = [(order[i], order[(i + by) % chips]) for i in range(chips)]
    return lax.ppermute(block, "tok", [(2 * a + c, 2 * b + c) for a, b in pairs for c in (0, 1)])


def ring_gather(halves, chips):
    blocks, ahead, behind = [list(halves)], list(halves), list(halves)
    for _ in range(chips // 2 - 1):
        for i in range(2):
            ahead[i] = shift(ahead[i], 1, chips)
            behind[i] = shift(behind[i], -1, chips)
        blocks += [list(ahead), list(behind)]
    blocks.append([shift(ahead[0], 1, chips), shift(behind[1], -1, chips)])
    return blocks


def halve_kernel(ahead_ref, behind_ref, upper_ref, lower_ref):
    half = upper_ref.shape[0]
    upper_ref[...] = ahead_ref[:half]
    lower_ref[...] = behind_ref[half:]


def ring_whole(block, chips):
    blocks, ahead, behind = [[block]], block, block
    for _ in range(chips // 2 - 1):
        ahead, behind = shift(ahead, 1, chips), shift(behind, -1, chips)
        blocks += [[ahead], [behind]]
    rows, width = block.shape
    upper, lower = call(halve_kernel, [shape((rows // 2, width), BF16)] * 2, [], [ahead, behind])
    blocks.append([shift(upper, 1, chips), shift(lower, -1, chips)])
    return blocks


def tie(arrays, others):
    return lax.optimization_barrier((arrays, others))[0]


def ring_offsets(chips):
    near = [sign * step for step in range(1, chips // 2) for sign in (-1, 1)]
    return [0] + near + [chips // 2]


def align_kernel(order_ref, rows_ref, out_ref):
    count = rows_ref.shape[0]
    picks = lax.broadcasted_iota(jnp.int32, (count, count), 0) == order_ref[...]
    out_ref[...] = contract(picks.astype(BF16), rows_ref[...], 0, 0).astype(BF16)


def cut_kernel(chips, rows_ref, out_ref):
    cols = out_ref.shape[2]
    for chip in range(chips):
        out_ref[chip] = rows_ref[:, chip * cols : (chip + 1) * cols]


def fold(rows, groups):
    size = rows.shape[0] // groups
    return [rows[i * size : (i + 1) * size] for i in range(groups)]


def pack_kernel(chips, count, keep_ref, come_ref, early_ref, late_ref, *outs):
    first_ref, second_ref, *streams = outs
    slab, half = first_ref.shape
    groups, offsets = chips // 2, ring_offsets(chips)
    own = (keep_ref[...] + come_ref[...].astype(F32)).astype(BF16)
    cols = half // groups
    blocks = [early_ref[i : i + count] for i in range(0, early_ref.shape[0], count)]
    blocks += [late_ref[i : i + count] for i in range(0, late_ref.shape[0], count)]
    for ref, (sign, side) in zip(streams, STREAMS, strict=True):
        ref[:slab] = own[:, side * half : (side + 1) * half]
        last = chips // 2 if (sign == 1) == (side == 0) else chips // 2 - 1
        row = slab
        for step in range(last, 0, -1):
            block = blocks[offsets.index(sign * step if step < chips // 2 else step)]
            parts = fold(block[side * count // 2 : (side + 1) * count // 2], groups)
            for i, part in enumerate(parts):
                ref[row : row + part.shape[0], i * cols : (i + 1) * cols] = part
            row += parts[0].shape[0]
    first_ref[...] = own[:, :half]
    second_ref[...] = own[:, half:]


def trim_kernel(message_ref, block_ref, piece_ref, *rest_ref):
    slab, size = block_ref.shape[0], piece_ref.shape[0]
    rest = message_ref.shape[0] - size
    block_ref[...] = message_ref[:slab]
    piece_ref[...] = message_ref[rest:]
    for ref in rest_ref:
        ref[...] = message_ref[:rest]


def join_kernel(chips, slab, places, first_ref, *refs):
    pieces, out_ref, held = refs[:-2], refs[-2], refs[-1]
    _, _, position = me(chips)
    count, cols = held.shape[1:]
    groups = chips // 2
    size = count // 2 // groups
    held[chip_at(position, chips)] = first_ref[...]
    for ref, (offset, side) in zip(pieces, places, strict=True):
        chip = chip_at((position + offset + chips) % chips, chips)
        piece = ref[ref.shape[0] - size :]
        for j in range(groups):
            base = side * count // 2 + j * size
            held[chip, base : base + size, :] = piece[:, j * cols : (j + 1) * cols]
    for chip in range(chips):
        out_ref[:, chip * cols : (chip + 1) * cols] = held[chip]


def rotate_kernel(count, chips, *refs):
    halves = refs[:count]
    if len(refs) == count + 2:
        cols_ref, out_ref = refs[count:]
    else:
        own_ref, sibling_ref, out_ref, cols_ref = refs[count:]
        _, core, _ = me(chips)
        slab = own_ref.shape[0] // chips
        for chip in range(chips):
            for ref, parity in ((own_ref, core), (sibling_ref, 1 - core)):
                row = pl.multiple_of((2 * chip + parity) * slab, 16)
                cols_ref[pl.ds(row, slab), :] = ref[chip * slab : (chip + 1) * slab, :]
    at = 0
    for half in halves:
        out_ref[at : at + half.shape[0], :] = jnp.dot(
            half[...], cols_ref[...], preferred_element_type=F32
        ).astype(BF16)
        at += half.shape[0]


def cov_sum(halves, groups, cons_ref, rows_ref):
    at = 0
    for half in halves:
        rows_ref[at : at + half.shape[0], :] = half[...]
        at += half.shape[0]
    at = 0
    for parts in groups:
        total = parts[0][...].astype(F32)
        for part in parts[1:]:
            total = total + part[...].astype(F32)
        cons_ref[at : at + total.shape[0], :] = (total / len(parts)).astype(BF16)
        at += total.shape[0]
    return contract(cons_ref[...], rows_ref[...], 0, 0)


def early_kernel(count, members, *refs):
    halves, near = refs[:count], refs[count : count + members]
    middle = refs[count + members : count + 2 * members]
    cons_ref, cov_ref, rows_ref = refs[count + 2 * members :]
    cov_ref[...] = cov_sum(halves, [near, middle], cons_ref, rows_ref)


def late_kernel(count, members, *refs):
    core = lax.axis_index("tok") % 2
    halves, far = refs[:count], refs[count : count + members]
    early_ref, cons_ref, keep_ref, give_ref, rows_ref = refs[count + members :]
    cov = early_ref[...] + cov_sum(halves, [far], cons_ref, rows_ref)
    slab = cov.shape[0] // 2
    low, high = cov[:slab], cov[slab:]
    keep_ref[...] = jnp.where(core == 0, low, high)
    give_ref[...] = jnp.where(core == 0, high, low).astype(BF16)


def chain_kernel(count, slab, *refs):
    blocks = refs[: 2 * count]
    out_ref, whole, flipped, turned = refs[2 * count :]
    width = whole.shape[0]
    chips = width // slab // 2
    index, core, position = me(chips)
    size, half = width // count, width // 2
    squares = jnp.zeros((1, width), F32)
    for i in range(count):
        for side in range(2):
            whole[i * size : (i + 1) * size, side * half : (side + 1) * half] = blocks[2 * i + side][:size]
        values = whole[i * size : (i + 1) * size, :].astype(F32)
        squares = squares + jnp.sum(values * values, axis=0, keepdims=True)
    inverse = 1.0 / (2.0 * jnp.sqrt(jnp.sum(squares, axis=1, keepdims=True) / width + 1e-06))

    rows = turned.shape[1]
    span = min(rows + 128, width)
    first_row = index * slab
    window = jnp.minimum(first_row // 128, (width - span) // 128) * 128
    window = pl.multiple_of(window, 128)
    columns = whole[:, pl.ds(window, span)]
    picks = lax.broadcasted_iota(jnp.int32, (rows, span), 1) == (
        lax.broadcasted_iota(jnp.int32, (rows, span), 0) + (first_row - window)
    )
    own = contract(picks.astype(BF16), columns, 1, 1)
    start = (own * inverse).astype(BF16)

    flipped[...] = whole[...].T

    def apply_once(vector):
        inner = jnp.dot(vector.astype(BF16), whole[...], preferred_element_type=F32) * inverse
        return jnp.dot(inner.astype(BF16), flipped[...], preferred_element_type=F32) * inverse

    first = 1.5 * start.astype(F32) - 0.5 * apply_once(start)
    upper = 1.5 * first - 0.5 * apply_once(first)
    middle = apply_once(upper)
    cubic = 1.5 * middle - 0.5 * apply_once(middle)
    result = math.sqrt(width) * (1.5 * first - 0.5 * cubic)
    if count == 1:
        out_ref[...] = result[:slab].astype(BF16)
        return
    result = result.T
    for i in range(count):
        chip = chip_at((position + ring_offsets(chips)[i % chips] + chips) % chips, chips)
        parity = core if i < chips else 1 - core
        row = pl.multiple_of((2 * chip + parity) * size, 16)
        turned[pl.ds(row, size), :] = result[i * size : (i + 1) * size, :]
    out_ref[...] = turned[...].T[:slab].astype(BF16)


def shards(features, pairing, rotation):
    own_rows, own_order, rot_rows = features[0], pairing[0], rotation[0]
    count, width = own_rows.shape
    devices, members = lax.axis_size("tok"), lax.axis_size("ckpt")
    chips = devices // 2
    slab, cols = width // devices, width // chips
    siblings = [(i, i ^ 1) for i in range(devices)]
    parity = [[2 * i + c for i in range(chips)] for c in (0, 1)]
    pairs = [[2 * i, 2 * i + 1] for i in range(chips)]
    offsets = ring_offsets(chips)
    tiled = slab % 16 == 0 and count % (16 * chips) == 0

    aligned = call(align_kernel, shape((count, width), BF16), [], [own_order, own_rows])
    blocks = ring_whole(aligned, chips)

    pieces = call(
        functools.partial(cut_kernel, chips), shape((chips, slab, cols), BF16), [], [rot_rows]
    )
    pieces = lax.all_to_all(
        pieces, "tok", split_axis=0, concat_axis=0, tiled=True, axis_index_groups=parity
    )
    if tiled:
        stacked = pieces.reshape(chips * slab, cols)
        rot_cols = [stacked, lax.ppermute(stacked, "tok", siblings)]
        rot_scratch = [shape((width, cols), BF16)]
    else:
        pieces = lax.all_gather(pieces, "tok", axis=1, axis_index_groups=pairs)
        rot_cols, rot_scratch = [pieces.reshape(width, cols)], []

    def rotate(group):
        halves = sum(group, [])
        rotated = call(
            functools.partial(rotate_kernel, len(halves), chips),
            shape((len(group) * count, cols), BF16),
            [],
            halves + rot_cols,
            rot_scratch,
            flops=2 * len(group) * count * cols * width,
        )
        if members == 2:
            return halves, [rotated, lax.ppermute(rotated, "ckpt", [(0, 1), (1, 0)])]
        gathered = lax.all_gather(rotated, "ckpt", axis=0)
        return halves, [gathered[i] for i in range(members)]

    early_rows, early_parts = rotate(blocks[:-3])
    middle_rows, middle_parts = rotate(blocks[-3:-1])
    far_rows, far_parts = rotate(blocks[-1:])
    near = (chips - 1) * count
    early_rows = early_rows + middle_rows
    early_cons, early_cov = call(
        functools.partial(early_kernel, len(early_rows), members),
        (shape((near, cols), BF16), shape((cols, width), F32)),
        [],
        early_rows + early_parts + middle_parts,
        [shape((near, width), BF16)],
        flops=2 * near * cols * width,
    )
    late_rows = far_rows
    late_cons, keep, give = call(
        functools.partial(late_kernel, len(late_rows), members),
        (shape((count, cols), BF16), shape((slab, width), F32), shape((slab, width), BF16)),
        [],
        late_rows + far_parts + [early_cov],
        [shape((count, width), BF16)],
        flops=2 * count * cols * width,
    )
    come = lax.ppermute(give, "tok", siblings)

    if tiled:
        half, last = width // 2, chips // 2 - 1
        size = count // chips
        sizes = [slab + size * (last + (sign == 1) * (side == 0) + (sign == -1) * (side == 1)) for sign, side in STREAMS]
        first, second, *streams = call(
            functools.partial(pack_kernel, chips, count),
            [shape((slab, half), BF16)] * 2 + [shape((rows, half), BF16) for rows in sizes],
            [],
            [keep, come, early_cons, late_cons],
        )
        same, pieces, places = [[first, second]], [], []
        for step in range(1, last + 1):
            parts = []
            for i, (sign, side) in enumerate(STREAMS):
                message = shift(streams[i], sign, chips)
                outs = [shape((rows, half), BF16) for rows in (slab, size, message.shape[0] - size)]
                if outs[2].shape == outs[0].shape:
                    outs = outs[:2]
                block, piece, *rest = call(trim_kernel, outs, [], [message])
                streams[i] = rest[0] if rest else block
                parts.append(block)
                pieces.append(piece)
                places.append((-sign * step, side))
            same += [parts[:2], parts[2:]]
        far = [shift(streams[0], 1, chips), shift(streams[3], -1, chips)]
        same.append(far)
        pieces += far
        places += [(chips // 2, 0), (chips // 2, 1)]
        other = [[lax.ppermute(part, "tok", siblings) for part in block] for block in same]
        gathered = sum(same + other, [])
    else:
        own = (keep + come.astype(F32)).astype(BF16)
        gathered = jnp.split(lax.all_gather(own, "tok", axis=0, tiled=True), 2, axis=1)
    rows = -(-slab // 128) * 128
    rotation_next = call(
        functools.partial(chain_kernel, len(gathered) // 2, slab),
        shape((slab, width), BF16),
        [],
        gathered,
        [shape((width, width), BF16)] * 2 + [shape((width, rows), F32)],
        flops=16 * rows * width * width,
        room=10,
    )

    if tiled:
        consensus = call(
            functools.partial(join_kernel, chips, slab, places),
            shape((count, width), BF16),
            [],
            [early_cons[:count]] + pieces,
            [shape((chips, count, cols), BF16)],
        )
    else:
        cons = jnp.concatenate([early_cons, late_cons]).reshape(chips, count, cols)
        _, _, position = me(chips)
        natural = jnp.stack([chip_at((position + offset + chips) % chips, chips) for offset in offsets])
        ordered = jnp.zeros((chips, count, cols), BF16).at[natural].set(cons, unique_indices=True)
        consensus = lax.all_to_all(
            ordered, "tok", split_axis=0, concat_axis=0, tiled=True, axis_index_groups=parity
        )
        consensus = consensus.transpose(1, 0, 2).reshape(count, width)
    return (consensus, rotation_next[None])


def solution(mesh):
    placed = (P("ckpt", "tok", None), P("ckpt", "tok", None), P("ckpt", "tok", None))
    return jax.shard_map(
        shards,
        mesh=mesh,
        in_specs=placed,
        out_specs=(P("tok", None), P("ckpt", "tok", None)),
        check_vma=False,
    )
```

```python
import functools
import math

import jax
import jax.numpy as jnp
from jax import lax
from jax.experimental import pallas as pl
from jax.experimental.pallas import tpu as pltpu
from jax.sharding import PartitionSpec as P

BF16 = jnp.bfloat16
F32 = jnp.float32
STREAMS = ((1, 0), (1, 1), (-1, 0), (-1, 1))
VMEM = pl.BlockSpec(memory_space=pltpu.VMEM)
SMEM = pl.BlockSpec(memory_space=pltpu.SMEM)


def shape(dims, dtype):
    return jax.ShapeDtypeStruct(dims, dtype)


def contract(left, right, left_dim, right_dim):
    return lax.dot_general(
        left, right, (((left_dim,), (right_dim,)), ((), ())), preferred_element_type=F32
    )


def nbytes(array):
    return math.prod(array.shape) * jnp.dtype(array.dtype).itemsize


def call(kernel, outs, smem, vmem, scratch=(), flops=0, room=4):
    held = sum(map(nbytes, [*vmem, *jax.tree.leaves(outs), *scratch]))
    return pl.pallas_call(
        kernel,
        out_shape=outs,
        in_specs=[SMEM] * len(smem) + [VMEM] * len(vmem),
        out_specs=jax.tree.map(lambda _: VMEM, outs),
        scratch_shapes=[pltpu.VMEM(s.shape, s.dtype) for s in scratch],
        compiler_params=pltpu.CompilerParams(vmem_limit_bytes=held + room * 2**20),
        cost_estimate=pl.CostEstimate(flops=flops, bytes_accessed=held, transcendentals=0),
    )(*smem, *vmem)


def position_of(chip, chips):
    return jnp.where(chip % 2 == 0, chip // 2, chips - 1 - chip // 2)


def chip_at(position, chips):
    return jnp.where(position < chips // 2, 2 * position, 2 * (chips - 1 - position) + 1)


def me(chips):
    index = lax.axis_index("tok")
    return index, index % 2, position_of(index // 2, chips)


def ring_order(chips):
    return list(range(0, chips, 2)) + list(range(chips - 1, 0, -2))


def shift(block, by, chips):
    order = ring_order(chips)
    pairs = [(order[i], order[(i + by) % chips]) for i in range(chips)]
    return lax.ppermute(block, "tok", [(2 * a + c, 2 * b + c) for a, b in pairs for c in (0, 1)])


def ring_gather(halves, chips):
    blocks, ahead, behind = [list(halves)], list(halves), list(halves)
    for _ in range(chips // 2 - 1):
        for i in range(2):
            ahead[i] = shift(ahead[i], 1, chips)
            behind[i] = shift(behind[i], -1, chips)
        blocks += [list(ahead), list(behind)]
    blocks.append([shift(ahead[0], 1, chips), shift(behind[1], -1, chips)])
    return blocks


def halve_kernel(ahead_ref, behind_ref, upper_ref, lower_ref):
    half = upper_ref.shape[0]
    upper_ref[...] = ahead_ref[:half]
    lower_ref[...] = behind_ref[half:]


def ring_whole(block, chips):
    blocks, ahead, behind = [[block]], block, block
    for _ in range(chips // 2 - 1):
        ahead, behind = shift(ahead, 1, chips), shift(behind, -1, chips)
        blocks += [[ahead], [behind]]
    rows, width = block.shape
    upper, lower = call(halve_kernel, [shape((rows // 2, width), BF16)] * 2, [], [ahead, behind])
    blocks.append([shift(upper, 1, chips), shift(lower, -1, chips)])
    return blocks


def tie(arrays, others):
    return lax.optimization_barrier((arrays, others))[0]


def ring_offsets(chips):
    near = [sign * step for step in range(1, chips // 2) for sign in (-1, 1)]
    return [0] + near + [chips // 2]


def align_kernel(order_ref, rows_ref, out_ref):
    count = rows_ref.shape[0]
    picks = lax.broadcasted_iota(jnp.int32, (count, count), 0) == order_ref[...]
    out_ref[...] = contract(picks.astype(BF16), rows_ref[...], 0, 0).astype(BF16)


def cut_kernel(chips, rows_ref, out_ref):
    cols = out_ref.shape[2]
    for chip in range(chips):
        out_ref[chip] = rows_ref[:, chip * cols : (chip + 1) * cols]


def fold(rows, groups):
    size = rows.shape[0] // groups
    return [rows[i * size : (i + 1) * size] for i in range(groups)]


def pack_kernel(chips, count, keep_ref, come_ref, early_ref, late_ref, *outs):
    first_ref, second_ref, *streams = outs
    slab, half = first_ref.shape
    groups, offsets = chips // 2, ring_offsets(chips)
    own = (keep_ref[...] + come_ref[...].astype(F32)).astype(BF16)
    cols = half // groups
    blocks = [early_ref[i : i + count] for i in range(0, early_ref.shape[0], count)]
    blocks += [late_ref[i : i + count] for i in range(0, late_ref.shape[0], count)]
    for ref, (sign, side) in zip(streams, STREAMS, strict=True):
        ref[:slab] = own[:, side * half : (side + 1) * half]
        last = chips // 2 if (sign == 1) == (side == 0) else chips // 2 - 1
        row = slab
        for step in range(last, 0, -1):
            block = blocks[offsets.index(sign * step if step < chips // 2 else step)]
            parts = fold(block[side * count // 2 : (side + 1) * count // 2], groups)
            for i, part in enumerate(parts):
                ref[row : row + part.shape[0], i * cols : (i + 1) * cols] = part
            row += parts[0].shape[0]
    first_ref[...] = own[:, :half]
    second_ref[...] = own[:, half:]


def trim_kernel(message_ref, block_ref, piece_ref, *rest_ref):
    slab, size = block_ref.shape[0], piece_ref.shape[0]
    rest = message_ref.shape[0] - size
    block_ref[...] = message_ref[:slab]
    piece_ref[...] = message_ref[rest:]
    for ref in rest_ref:
        ref[...] = message_ref[:rest]


def join_kernel(chips, slab, places, first_ref, *refs):
    pieces, out_ref, held = refs[:-2], refs[-2], refs[-1]
    _, _, position = me(chips)
    count, cols = held.shape[1:]
    groups = chips // 2
    size = count // 2 // groups
    held[chip_at(position, chips)] = first_ref[...]
    for ref, (offset, side) in zip(pieces, places, strict=True):
        chip = chip_at((position + offset + chips) % chips, chips)
        piece = ref[ref.shape[0] - size :]
        for j in range(groups):
            base = side * count // 2 + j * size
            held[chip, base : base + size, :] = piece[:, j * cols : (j + 1) * cols]
    for chip in range(chips):
        out_ref[:, chip * cols : (chip + 1) * cols] = held[chip]


def rotate_kernel(count, chips, *refs):
    halves = refs[:count]
    if len(refs) == count + 2:
        cols_ref, out_ref = refs[count:]
    else:
        own_ref, sibling_ref, out_ref, cols_ref = refs[count:]
        _, core, _ = me(chips)
        slab = own_ref.shape[0] // chips
        for chip in range(chips):
            for ref, parity in ((own_ref, core), (sibling_ref, 1 - core)):
                row = pl.multiple_of((2 * chip + parity) * slab, 16)
                cols_ref[pl.ds(row, slab), :] = ref[chip * slab : (chip + 1) * slab, :]
    at = 0
    for half in halves:
        out_ref[at : at + half.shape[0], :] = jnp.dot(
            half[...], cols_ref[...], preferred_element_type=F32
        ).astype(BF16)
        at += half.shape[0]


def cov_sum(halves, groups, cons_ref, rows_ref):
    at = 0
    for half in halves:
        rows_ref[at : at + half.shape[0], :] = half[...]
        at += half.shape[0]
    at = 0
    for parts in groups:
        total = parts[0][...].astype(F32)
        for part in parts[1:]:
            total = total + part[...].astype(F32)
        cons_ref[at : at + total.shape[0], :] = (total / len(parts)).astype(BF16)
        at += total.shape[0]
    return contract(cons_ref[...], rows_ref[...], 0, 0)


def early_kernel(count, members, *refs):
    halves, near = refs[:count], refs[count : count + members]
    middle = refs[count + members : count + 2 * members]
    cons_ref, cov_ref, rows_ref = refs[count + 2 * members :]
    cov_ref[...] = cov_sum(halves, [near, middle], cons_ref, rows_ref)


def late_kernel(count, members, *refs):
    core = lax.axis_index("tok") % 2
    halves, far = refs[:count], refs[count : count + members]
    early_ref, cons_ref, keep_ref, give_ref, rows_ref = refs[count + members :]
    cov = early_ref[...] + cov_sum(halves, [far], cons_ref, rows_ref)
    slab = cov.shape[0] // 2
    low, high = cov[:slab], cov[slab:]
    keep_ref[...] = jnp.where(core == 0, low, high)
    give_ref[...] = jnp.where(core == 0, high, low).astype(BF16)


def chain_kernel(count, slab, *refs):
    blocks = refs[: 2 * count]
    out_ref, whole, flipped, turned = refs[2 * count :]
    width = whole.shape[0]
    chips = width // slab // 2
    index, core, position = me(chips)
    size, half = width // count, width // 2
    squares = jnp.zeros((1, width), F32)
    for i in range(count):
        for side in range(2):
            whole[i * size : (i + 1) * size, side * half : (side + 1) * half] = blocks[2 * i + side][:size]
        values = whole[i * size : (i + 1) * size, :].astype(F32)
        squares = squares + jnp.sum(values * values, axis=0, keepdims=True)
    inverse = 1.0 / (2.0 * jnp.sqrt(jnp.sum(squares, axis=1, keepdims=True) / width + 1e-06))

    rows = turned.shape[1]
    span = min(rows + 128, width)
    first_row = index * slab
    window = jnp.minimum(first_row // 128, (width - span) // 128) * 128
    window = pl.multiple_of(window, 128)
    columns = whole[:, pl.ds(window, span)]
    picks = lax.broadcasted_iota(jnp.int32, (rows, span), 1) == (
        lax.broadcasted_iota(jnp.int32, (rows, span), 0) + (first_row - window)
    )
    own = contract(picks.astype(BF16), columns, 1, 1)
    start = (own * inverse).astype(BF16)

    def apply_once(vector):
        inner = jnp.dot(vector.astype(BF16), whole[...], preferred_element_type=F32) * inverse
        return jnp.dot(inner.astype(BF16), flipped[...], preferred_element_type=F32) * inverse

    inner = jnp.dot(start, whole[...], preferred_element_type=F32) * inverse
    flipped[...] = whole[...].T
    applied = jnp.dot(inner.astype(BF16), flipped[...], preferred_element_type=F32) * inverse
    first = 1.5 * start.astype(F32) - 0.5 * applied
    upper = 1.5 * first - 0.5 * apply_once(first)
    middle = apply_once(upper)
    cubic = 1.5 * middle - 0.5 * apply_once(middle)
    result = math.sqrt(width) * (1.5 * first - 0.5 * cubic)
    if count == 1:
        out_ref[...] = result[:slab].astype(BF16)
        return
    result = result.T
    for i in range(count):
        chip = chip_at((position + ring_offsets(chips)[i % chips] + chips) % chips, chips)
        parity = core if i < chips else 1 - core
        row = pl.multiple_of((2 * chip + parity) * size, 16)
        turned[pl.ds(row, size), :] = result[i * size : (i + 1) * size, :]
    out_ref[...] = turned[...].T[:slab].astype(BF16)


def shards(features, pairing, rotation):
    own_rows, own_order, rot_rows = features[0], pairing[0], rotation[0]
    count, width = own_rows.shape
    devices, members = lax.axis_size("tok"), lax.axis_size("ckpt")
    chips = devices // 2
    slab, cols = width // devices, width // chips
    siblings = [(i, i ^ 1) for i in range(devices)]
    parity = [[2 * i + c for i in range(chips)] for c in (0, 1)]
    pairs = [[2 * i, 2 * i + 1] for i in range(chips)]
    offsets = ring_offsets(chips)
    tiled = slab % 16 == 0 and count % (16 * chips) == 0

    aligned = call(align_kernel, shape((count, width), BF16), [], [own_order, own_rows])
    blocks = ring_whole(aligned, chips)

    pieces = call(
        functools.partial(cut_kernel, chips), shape((chips, slab, cols), BF16), [], [rot_rows]
    )
    pieces = lax.all_to_all(
        pieces, "tok", split_axis=0, concat_axis=0, tiled=True, axis_index_groups=parity
    )
    if tiled:
        stacked = pieces.reshape(chips * slab, cols)
        rot_cols = [stacked, lax.ppermute(stacked, "tok", siblings)]
        rot_scratch = [shape((width, cols), BF16)]
    else:
        pieces = lax.all_gather(pieces, "tok", axis=1, axis_index_groups=pairs)
        rot_cols, rot_scratch = [pieces.reshape(width, cols)], []

    def rotate(group):
        halves = sum(group, [])
        rotated = call(
            functools.partial(rotate_kernel, len(halves), chips),
            shape((len(group) * count, cols), BF16),
            [],
            halves + rot_cols,
            rot_scratch,
            flops=2 * len(group) * count * cols * width,
        )
        if members == 2:
            return halves, [rotated, lax.ppermute(rotated, "ckpt", [(0, 1), (1, 0)])]
        gathered = lax.all_gather(rotated, "ckpt", axis=0)
        return halves, [gathered[i] for i in range(members)]

    early_rows, early_parts = rotate(blocks[:-3])
    middle_rows, middle_parts = rotate(blocks[-3:-1])
    far_rows, far_parts = rotate(blocks[-1:])
    near = (chips - 1) * count
    early_rows = early_rows + middle_rows
    early_cons, early_cov = call(
        functools.partial(early_kernel, len(early_rows), members),
        (shape((near, cols), BF16), shape((cols, width), F32)),
        [],
        early_rows + early_parts + middle_parts,
        [shape((near, width), BF16)],
        flops=2 * near * cols * width,
    )
    late_rows = far_rows
    late_cons, keep, give = call(
        functools.partial(late_kernel, len(late_rows), members),
        (shape((count, cols), BF16), shape((slab, width), F32), shape((slab, width), BF16)),
        [],
        late_rows + far_parts + [early_cov],
        [shape((count, width), BF16)],
        flops=2 * count * cols * width,
    )
    come = lax.ppermute(give, "tok", siblings)

    if tiled:
        half, last = width // 2, chips // 2 - 1
        size = count // chips
        sizes = [slab + size * (last + (sign == 1) * (side == 0) + (sign == -1) * (side == 1)) for sign, side in STREAMS]
        first, second, *streams = call(
            functools.partial(pack_kernel, chips, count),
            [shape((slab, half), BF16)] * 2 + [shape((rows, half), BF16) for rows in sizes],
            [],
            [keep, come, early_cons, late_cons],
        )
        same, pieces, places = [[first, second]], [], []
        for step in range(1, last + 1):
            parts = []
            for i, (sign, side) in enumerate(STREAMS):
                message = shift(streams[i], sign, chips)
                outs = [shape((rows, half), BF16) for rows in (slab, size, message.shape[0] - size)]
                if outs[2].shape == outs[0].shape:
                    outs = outs[:2]
                block, piece, *rest = call(trim_kernel, outs, [], [message])
                streams[i] = rest[0] if rest else block
                parts.append(block)
                pieces.append(piece)
                places.append((-sign * step, side))
            same += [parts[:2], parts[2:]]
        far = [shift(streams[0], 1, chips), shift(streams[3], -1, chips)]
        same.append(far)
        pieces += far
        places += [(chips // 2, 0), (chips // 2, 1)]
        other = [[lax.ppermute(part, "tok", siblings) for part in block] for block in same]
        gathered = sum(same + other, [])
    else:
        own = (keep + come.astype(F32)).astype(BF16)
        gathered = jnp.split(lax.all_gather(own, "tok", axis=0, tiled=True), 2, axis=1)
    rows = -(-slab // 128) * 128
    rotation_next = call(
        functools.partial(chain_kernel, len(gathered) // 2, slab),
        shape((slab, width), BF16),
        [],
        gathered,
        [shape((width, width), BF16)] * 2 + [shape((width, rows), F32)],
        flops=16 * rows * width * width,
        room=10,
    )

    if tiled:
        consensus = call(
            functools.partial(join_kernel, chips, slab, places),
            shape((count, width), BF16),
            [],
            [early_cons[:count]] + pieces,
            [shape((chips, count, cols), BF16)],
        )
    else:
        cons = jnp.concatenate([early_cons, late_cons]).reshape(chips, count, cols)
        _, _, position = me(chips)
        natural = jnp.stack([chip_at((position + offset + chips) % chips, chips) for offset in offsets])
        ordered = jnp.zeros((chips, count, cols), BF16).at[natural].set(cons, unique_indices=True)
        consensus = lax.all_to_all(
            ordered, "tok", split_axis=0, concat_axis=0, tiled=True, axis_index_groups=parity
        )
        consensus = consensus.transpose(1, 0, 2).reshape(count, width)
    return (consensus, rotation_next[None])


def solution(mesh):
    placed = (P("ckpt", "tok", None), P("ckpt", "tok", None), P("ckpt", "tok", None))
    return jax.shard_map(
        shards,
        mesh=mesh,
        in_specs=placed,
        out_specs=(P("tok", None), P("ckpt", "tok", None)),
        check_vma=False,
    )
```
